128 devices in a mesh: guide: 2 (over core), frame: 64 (over z, x, y).
Axes of the slice: x: 4, y: 4, z: 4, core: 2. Of those that a mesh axis runs over, the one named last changes fastest.
Arguments:
- head_labels: int32 [24], replicated, may hold values from 0 to 1, as said below
- queries: bfloat16 [2, 32768, 3072], P('guide', 'frame'), may hold values from -5 to 5
- key_heads: bfloat16 [2, 32768, 3072], P('guide', 'frame'), may hold values from -5 to 5
- value_heads: bfloat16 [2, 32768, 3072], P('guide', 'frame'), may hold values from -6 to 6
- hidden_state: bfloat16 [2, 32768, 3072], P('guide', 'frame'), may hold values from -2 to 2
- gate_scale: float32 [2, 3072], replicated, may hold values from 0.5 to 4
- out_weight: bfloat16 [3072, 3072], P(None, ('guide', 'frame')), may hold values from -0.109375 to 0.109375
- final_scale: float32 [2, 3072], replicated, may hold values from -2.5 to 2.5
- final_shift: float32 [2, 3072], replicated, may hold values from -2.5 to 2.5
- final_weight: bfloat16 [3072, 64], replicated, may hold values from -0.109375 to 0.109375
- latent: float32 [32768, 64], P('frame', 'guide'), may hold values from -6 to 6
Outputs:
- latent_next: float32 [32768, 64], P('frame', 'guide')
The draws below stay inside these ranges and needn't reach their ends.
Inputs may be any that keep to these rules, and one draw needn't show every extreme that they name: `head_labels`: exactly 12 entries are 1; which heads they are varies from draw to draw.
All inputs are finite; a program needn't handle non-finite values.
Results may differ from the reference program's by a relative error of at most 0.005.
Values may be sent and summed in bfloat16 or wider, within the bound.
A program may use at most 128 MiB of HBM per device.

```python
import math
import jax
import jax.numpy as jnp
from jax import lax

H = 24
HD = 128
OUT_CH = 64
NT = 12
TPF = 512
D = 3072
FRAMES = 64
TOKENS = 32768


def draw_head_labels(key, part):
    key = jax.random.fold_in(key, 1)
    order = jax.random.permutation(key, H)
    return (order < NT).astype(jnp.int32)


def draw_queries(key, part):
    key = jax.random.fold_in(key, 2)
    key_base = jax.random.fold_in(key, 0)
    base = jnp.clip(jax.random.normal(key_base, (2, FRAMES, TPF, D), jnp.float32), -4.8, 4.8)
    return base.reshape(2, TOKENS, D).astype(jnp.bfloat16)


def draw_key_heads(key, part):
    key = jax.random.fold_in(key, 3)
    key_base = jax.random.fold_in(key, 0)
    base = jnp.clip(jax.random.normal(key_base, (2, FRAMES, TPF, D), jnp.float32), -4.8, 4.8)
    return base.reshape(2, TOKENS, D).astype(jnp.bfloat16)


def block_levels(stream_key, dims, cuts, low, top_value):
    loudness, own = 1.0, jax.random.fold_in(stream_key, 6)
    for dim, parts in cuts:
        draws = jnp.exp(jax.random.uniform(jax.random.fold_in(own, dim), (parts,), jnp.float32, low / len(cuts), top_value / len(cuts)))
        loudness = loudness * jnp.repeat(draws, dims[dim] // parts).reshape([-1 if axis == dim else 1 for axis in range(len(dims))])
    return loudness


def scatter_about(rng, dims, spread, limit, cuts=(), held_as=jnp.bfloat16):
    result = jax.random.normal(rng, dims, jnp.float32) * spread
    if len(cuts) > 0:
        result = block_levels(rng, dims, cuts, -0.22, 0.18) * result
    return jnp.clip(result, min=-limit, max=limit).astype(held_as)


def setup_inputs(seed: int = 0) -> dict:
    key_of = jax.random.split(jax.random.key(seed), 12)
    head_labels = draw_head_labels(jax.random.fold_in(key_of[11], 71), 0)
    queries = draw_queries(jax.random.fold_in(key_of[11], 71), 0)
    key_heads = draw_key_heads(jax.random.fold_in(key_of[11], 71), 0)
    value_heads = scatter_about(key_of[3], (2, TOKENS, D), 1.0, 6.0, ((0, 2), (1, 64)))
    hidden_state = scatter_about(key_of[4], (2, TOKENS, D), 0.3, 2.0, ((0, 2), (1, 64)))
    gate_scale = jnp.clip(jnp.exp(jax.random.uniform(key_of[5], (2, D), jnp.float32, math.log(0.5), math.log(4.0))), 0.5, 4.0)
    out_weight = scatter_about(key_of[6], (D, D), D ** -0.5, 0.109375, ((1, 128),))
    final_scale = scatter_about(key_of[7], (2, D), 0.5, 2.5, (), jnp.float32)
    final_shift = scatter_about(key_of[8], (2, D), 0.5, 2.5, (), jnp.float32)
    final_weight = scatter_about(key_of[9], (D, OUT_CH), D ** -0.5, 0.109375)
    latent = scatter_about(key_of[10], (TOKENS, OUT_CH), 1.0, 6.0, ((0, 64), (1, 2)), jnp.float32)
    return dict(head_labels=head_labels, queries=queries, key_heads=key_heads, value_heads=value_heads, hidden_state=hidden_state, gate_scale=gate_scale, out_weight=out_weight, final_scale=final_scale, final_shift=final_shift, final_weight=final_weight, latent=latent)


guidance = 6.0
euler_step = 0.25
norm_eps = 1e-06

def softmax_round(scores):
    top = lax.optimization_barrier(jnp.max(scores, axis=-1, keepdims=True))
    expd = jnp.exp(scores - top)
    return (expd / lax.optimization_barrier(jnp.sum(expd, axis=-1, keepdims=True))).astype(jnp.bfloat16)

def final_norm(mixed, scale_row, shift_row):
    wide = mixed.astype(jnp.float32)
    row_mean = lax.optimization_barrier(jnp.mean(wide, axis=-1, keepdims=True))
    row_square = lax.optimization_barrier(jnp.mean(wide * wide, axis=-1, keepdims=True))
    normed = (wide - row_mean) * lax.rsqrt(row_square - row_mean * row_mean + norm_eps)
    return (normed * (1.0 + scale_row[None, :]) + shift_row[None, :]).astype(jnp.bfloat16)

def reference(head_labels, queries, key_heads, value_heads, hidden_state, gate_scale, out_weight, final_scale, final_shift, final_weight, latent):
    scale = 1.0 / math.sqrt(HD)
    order_s = jnp.argsort(head_labels, stable=True)[:H - NT].astype(jnp.int32)
    order_t = jnp.argsort(1 - head_labels, stable=True)[:NT].astype(jnp.int32)
    q_view = queries.reshape(2, FRAMES, TPF, H, HD)
    k_view = key_heads.reshape(2, FRAMES, TPF, H, HD)
    v_view = value_heads.reshape(2, FRAMES, TPF, H, HD)

    def spatial_one(trio):
        qq, kk, vv = trio
        scores = jnp.einsum('qhd,khd->hqk', qq.astype(jnp.float32), kk.astype(jnp.float32)) * scale
        weights = softmax_round(scores)
        return jnp.einsum('hqk,khd->qhd', weights.astype(jnp.float32), vv.astype(jnp.float32)).astype(jnp.bfloat16)

    def pick(view, order):
        return jnp.take(view, order, axis=3)
    spat_in = tuple((pick(view, order_s).reshape(2 * FRAMES, TPF, H - NT, HD) for view in (q_view, k_view, v_view)))
    spatial = lax.map(spatial_one, spat_in).reshape(2, FRAMES, TPF, H - NT, HD)

    def temporal_one(trio):
        qq, kk, vv = trio
        scores = jnp.einsum('fphd,gphd->phfg', qq.astype(jnp.float32), kk.astype(jnp.float32)) * scale
        weights = softmax_round(scores)
        return jnp.einsum('phfg,gphd->fphd', weights.astype(jnp.float32), vv.astype(jnp.float32)).astype(jnp.bfloat16)
    temp_in = tuple((pick(view, order_t) for view in (q_view, k_view, v_view)))
    temporal = lax.map(temporal_one, temp_in)
    attended = jnp.zeros((2, FRAMES, TPF, H, HD), jnp.bfloat16)
    attended = attended.at[:, :, :, order_s].set(spatial).at[:, :, :, order_t].set(temporal)
    attended = attended.reshape(2, TOKENS, D)
    velocity = []
    for branch in range(2):
        projected = jnp.dot(attended[branch], out_weight, preferred_element_type=jnp.float32)
        mixed = (hidden_state[branch] + gate_scale[branch][None, :] * projected).astype(jnp.bfloat16)
        modulated = final_norm(mixed, final_scale[branch], final_shift[branch])
        velocity.append(jnp.dot(modulated, final_weight, preferred_element_type=jnp.float32))
    guided = velocity[1] + guidance * (velocity[0] - velocity[1])
    return latent - euler_step * guided
```

```python
import math

import jax
import jax.numpy as jnp
from jax import lax
from jax.experimental import pallas as pl
from jax.experimental.pallas import tpu as pltpu
from jax.sharding import PartitionSpec as P

H = 24
HD = 128
OUT_CH = 64
NT = 12
D = 3072
ROWS = 512
FRAMES = 64
HALF = D // 2
COLS = 24
GP = 16
NC = 2
JC = 3
QROWS = 3 * JC * GP
OROWS = JC * GP
PART = 1024
PLANE = 16 * COLS
MESH = pl.DeviceIdType.MESH
NTDOT = (((1,), (1,)), ((), ()))
NNDOT = (((1,), (0,)), ((), ()))

guidance = 6.0
euler_step = 0.25
norm_eps = 1e-06
SCORE_SCALE = 1.0 / math.sqrt(HD)


def dot(a, b, dims):
    return lax.dot_general(a, b, dims, preferred_element_type=jnp.float32)


def order_of(labels):
    index = jnp.arange(H, dtype=jnp.int32)
    before = jnp.sum(jnp.where(index[None, :] < index[:, None], labels[None, :], 0), axis=1)
    slot = jnp.where(labels == 0, index - before, NT + before)
    return jnp.sum(
        jnp.where(slot[None, :] == index[:, None], index[None, :], 0), axis=1, dtype=jnp.int32
    )


def lanes_of(head):
    return pl.ds(pl.multiple_of(head * HD, HD), HD)


def kernel(
    order, q_hbm, k_hbm, v_hbm, hid_hbm, w_hbm, f_ref, gate, scale, shift, out,
    qv, kv, vv, send, recv, osend, orecv, att, wsrc, wb, wch, hid, tmp, otmp, ft, consts,
    zacc, sacc, zrecv,
    load_sem, own_sem, qs_sem, qr_sem, os_sem, or_sem, w1s, w1r, w2s, w2r, w3s, w3r,
    part_s, part_r,
):
    g = lax.axis_index("guide")
    f = lax.axis_index("frame")
    z, x, y = f // 16, (f // 4) % 4, f % 4
    partner = (1 - g, f)

    def at(zz, xx, yy):
        return (g, (zz % 4) * 16 + (xx % 4) * 4 + yy % 4)

    def frame_of(i):
        a, b, c = i % 4, (i // 4) % 4, i // 16
        return ((z + a + c) % 4) * 16 + ((x + a + b) % 4) * 4 + (y + a) % 4

    def remote(src, dst, ssem, rsem, dev):
        return pltpu.make_async_remote_copy(
            src_ref=src, dst_ref=dst, send_sem=ssem, recv_sem=rsem,
            device_id=dev, device_id_type=MESH,
        )

    def wait_bytes(ref, sem):
        pltpu.make_async_copy(ref, ref, sem).wait()

    own_half = pl.ds(pl.multiple_of(g * HALF, HALF), HALF)
    other_half = pl.ds(pl.multiple_of((1 - g) * HALF, HALF), HALF)

    def load(h, carry):
        lanes = lanes_of(h)
        pltpu.make_async_copy(w_hbm.at[:, lanes], wsrc.at[h], load_sem.at[0]).start()
        for t, (src, dst) in enumerate(((q_hbm, qv), (k_hbm, kv), (v_hbm, vv))):
            pltpu.make_async_copy(src.at[0, :, lanes], dst.at[h], load_sem.at[1 + t]).start()
        return carry

    lax.fori_loop(0, H, load, 0)
    hid_in = pltpu.make_async_copy(hid_hbm.at[0, :, own_half], hid.at[g], load_sem.at[4])
    hid_in.start()

    bar = pltpu.get_barrier_semaphore()

    def greet(i, carry):
        pl.semaphore_signal(bar, inc=1, device_id=(g, frame_of(i)), device_id_type=MESH)
        return carry

    lax.fori_loop(1, FRAMES, greet, 0)
    pl.semaphore_signal(bar, inc=1, device_id=partner, device_id_type=MESH)

    wait_bytes(wsrc, load_sem.at[0])
    for part in range(3):
        def permute(i, carry, part=part):
            j = part * 8 + i
            h = order[j]
            wb[part, z, x, y, :, pl.ds(pl.multiple_of(i * HD, HD), HD)] = wsrc[h]
            return carry

        lax.fori_loop(0, 8, permute, 0)

    pl.semaphore_wait(bar, FRAMES)

    w1 = []
    for part in range(3):
        for k, step in enumerate((1, 3, 2)):
            dev = (at(z, x, y + step), at(z, x + step, y), at(z + step, x, y))[part]
            block = wb.at[part, z, x, y]
            w1.append(remote(block, block, w1s.at[part * 3 + k], w1r.at[part], dev))
    for c in w1:
        c.start()
    hid_out = remote(
        hid_hbm.at[0, :, other_half], hid.at[g], part_s.at[0], part_r.at[0], partner
    )
    hid_out.start()

    for t, ref in enumerate((qv, kv, vv)):
        wait_bytes(ref, load_sem.at[1 + t])
    for c in range(NC):
        def gather(i, carry, c=c):
            hh, jj = i // JC, i % JC
            h = order[NT + c * 2 * JC + i]
            for t, ref in enumerate((qv, kv, vv)):
                rows = pl.ds(pl.multiple_of((t * JC + jj) * GP, GP), GP)
                send[c, :, hh, rows, :] = ref[h].reshape(FRAMES // 2, GP, HD)
            return carry

        lax.fori_loop(0, 2 * JC, gather, 0)

        def post(i, carry, c=c):
            d = frame_of(i)
            remote(
                send.at[c, d // 2, d % 2], recv.at[c, f], qs_sem.at[c], qr_sem.at[c], (g, d)
            ).start()
            return carry

        lax.fori_loop(1, FRAMES, post, 0)
        pltpu.make_async_copy(send.at[c, f // 2, f % 2], recv.at[c, f], own_sem.at[c]).start()

    def softmax_av(scores, values):
        top = jnp.max(scores, axis=-1, keepdims=True)
        expd = jnp.exp((scores - top) * SCORE_SCALE)
        total = jnp.sum(expd, axis=-1, keepdims=True)
        return dot((expd * (1.0 / total)).astype(jnp.bfloat16), values, NNDOT)

    def spatial(js, carry):
        h = order[js]
        keys, values = kv[h], vv[h]
        out_lanes = pl.ds(pl.multiple_of(js * HD, HD), HD)
        for rb in range(4):
            rows = pl.ds(rb * 128, 128)
            scores = dot(qv[h, rows, :], keys, NTDOT)
            att[g, rows, out_lanes] = softmax_av(scores, values).astype(jnp.bfloat16)
        return carry

    lax.fori_loop(0, 4, spatial, 0)

    def stage2(part):
        if part == 0:
            return wb.at[0, z, x]
        if part == 1:
            return wb.at[1, z, :, y]
        return wb.at[2, :, x, y]

    w2 = []
    for part in range(3):
        wait_bytes(wb.at[part, 0, 0, pl.ds(0, 3)], w1r.at[part])
        for k, step in enumerate((1, 3, 2)):
            dev = (at(z, x + step, y), at(z + step, x, y), at(z, x, y + step))[part]
            c = remote(stage2(part), stage2(part), w2s.at[part * 3 + k], w2r.at[part], dev)
            c.start()
            w2.append(c)

    lax.fori_loop(4, NT, spatial, 0)
    half_s = att.at[g, :, pl.ds(0, HALF)]
    att_s = remote(half_s, half_s, part_s.at[1], part_r.at[1], partner)
    att_s.start()

    row_id = lax.broadcasted_iota(jnp.int32, (16, HALF), 0)
    ones_row = jnp.where(row_id == 0, 1.0, 0.0).astype(jnp.bfloat16)
    for b in range(2):
        own_scale = 1.0 + scale[pl.ds(b, 1), own_half]
        for base, who in ((0, g), (48, 1 - g)):
            chans = pl.ds(pl.multiple_of(who * 32, 32), 32)
            ft[b, pl.ds(base, 32), :] = (
                f_ref[chans, own_half].astype(jnp.float32) * own_scale
            ).astype(jnp.bfloat16)
            ft[b, pl.ds(base + 32, 16), :] = ones_row
        chans = pl.ds(pl.multiple_of(g * 32, 32), 32)
        wide = f_ref[chans, :].astype(jnp.float32)
        scaled = (wide * (1.0 + scale[pl.ds(b, 1), :])).astype(jnp.bfloat16).astype(jnp.float32)
        consts[b, 0] = jnp.broadcast_to(jnp.sum(scaled, axis=1, keepdims=True), (32, HD))
        consts[b, 1] = jnp.broadcast_to(
            jnp.sum(wide * shift[pl.ds(b, 1), :], axis=1, keepdims=True), (32, HD)
        )
    zacc[...] = jnp.zeros_like(zacc)
    sacc[...] = jnp.zeros_like(sacc)

    same = (
        lax.broadcasted_iota(jnp.int32, (128, 128), 0) // FRAMES
        == lax.broadcasted_iota(jnp.int32, (128, 128), 1) // FRAMES
    )
    for c in range(NC):
        wait_bytes(recv.at[c, pl.ds(0, FRAMES - 1)], qr_sem.at[c])
        pltpu.make_async_copy(send.at[c, f // 2, f % 2], recv.at[c, f], own_sem.at[c]).wait()

        def temporal(jj, carry, c=c):
            for t in range(3):
                rows = pl.ds(pl.multiple_of((t * JC + jj) * GP, GP), GP)
                tmp[t] = recv[c, :, rows, :].reshape(FRAMES * GP, HD).astype(jnp.float32)

            def two(t, pair):
                return jnp.concatenate(
                    [
                        tmp[t, pl.ds(2 * pair + i, FRAMES, stride=GP), :].astype(jnp.bfloat16)
                        for i in range(2)
                    ],
                    axis=0,
                )

            for pair in range(GP // 2):
                scores = jnp.where(same, dot(two(0, pair), two(1, pair), NTDOT), -1e30)
                result = softmax_av(scores, two(2, pair))
                for i in range(2):
                    otmp[pl.ds(2 * pair + i, FRAMES, stride=GP), :] = result[
                        i * FRAMES : (i + 1) * FRAMES
                    ]
            rows = pl.ds(pl.multiple_of(jj * GP, GP), GP)
            osend[c, :, rows, :] = otmp[...].astype(jnp.bfloat16).reshape(FRAMES, GP, HD)
            return carry

        lax.fori_loop(0, JC, temporal, 0)

        def reply(i, carry, c=c):
            d = frame_of(i)
            remote(
                osend.at[c, d], orecv.at[c, f // 2, f % 2], os_sem.at[c], or_sem.at[c], (g, d)
            ).start()
            return carry

        lax.fori_loop(1, FRAMES, reply, 0)
        pltpu.make_async_copy(
            osend.at[c, f], orecv.at[c, f // 2, f % 2], own_sem.at[NC + c]
        ).start()

    for part in range(3):
        wait_bytes(wb.at[part, 0, pl.ds(0, 3)], w2r.at[part])

    def plane_of(r):
        return (z + jnp.where(r == 2, 3, jnp.where(r == 3, 2, r))) % 4

    def neighbour(part, step):
        return (at(z + step, x, y), at(z, x, y + step), at(z, x + step, y))[part]

    def piece(part, r, step, keep):
        if part == 0:
            return wb.at[0, (z + step) % 4, r, keep]
        if part == 1:
            return wb.at[1, plane_of(r), keep, (y + step) % 4]
        return wb.at[2, plane_of(r), (x + step) % 4, keep]

    whole, first, last = pl.ds(0, 4), pl.ds(0, 2), pl.ds(2, 2)

    def direct(part, r, way):
        ref = piece(part, r, 0, whole)
        return remote(
            ref, ref, w3s.at[part, r, way], w3r.at[part, r, way],
            neighbour(part, (1, 3)[way]),
        )

    def forward(part, r, way):
        ref = piece(part, r, (3, 1)[way], (first, last)[way])
        return remote(
            ref, ref, w3s.at[part, r, 2 + way], w3r.at[part, r, 2 + way],
            neighbour(part, (1, 3)[way]),
        )

    def arrived(part, r):
        for way in range(2):
            wait_bytes(piece(part, r, (3, 1)[way], whole), w3r.at[part, r, way])

    def arrived_far(part, r):
        for way in range(2):
            wait_bytes(piece(part, r, 2, (first, last)[way]), w3r.at[part, r, 2 + way])

    def post_direct(part, r):
        for way in range(2):
            direct(part, r, way).start()

    def pass_on(part, r):
        arrived(part, r)
        for way in range(2):
            forward(part, r, way).start()

    for r in range(2):
        for part in range(3):
            post_direct(part, r)
    for r in range(2, 4):
        post_direct(0, r)

    for c in range(NC):
        wait_bytes(osend.at[c, pl.ds(0, FRAMES - 1)], or_sem.at[c])
        pltpu.make_async_copy(
            osend.at[c, f], orecv.at[c, f // 2, f % 2], own_sem.at[NC + c]
        ).wait()
        for i in range(2 * JC):
            hh, jj = i // JC, i % JC
            lanes = pl.ds(HALF + (c * 2 * JC + i) * HD, HD)
            att[g, :, lanes] = orecv[c, :, hh, pl.ds(jj * GP, GP), :].reshape(ROWS, HD)
        block = att.at[g, :, pl.ds(HALF + c * 2 * JC * HD, 2 * JC * HD)]
        remote(block, block, part_s.at[2 + c], part_r.at[2 + c], partner).start()

    hid_in.wait()
    hid_out.wait_recv()
    att_s.wait_recv()
    for c in range(NC):
        block = att.at[g, :, pl.ds(HALF + c * 2 * JC * HD, 2 * JC * HD)]
        remote(block, block, part_s.at[2 + c], part_r.at[2 + c], partner).wait_recv()

    for part in (1, 2):
        pass_on(part, 0)
        post_direct(part, 2)
    for r in range(2):
        pass_on(0, r)

    def project(r, carry):
        @pl.when(r < 4)
        def _():
            for part in (1, 2):
                pass_on(part, r)

        @pl.when(r == 1)
        def _():
            for part in (1, 2):
                post_direct(part, 3)

        @pl.when(r == 2)
        def _():
            for k in range(2, 4):
                pass_on(0, k)

        for part in (1, 2):
            arrived_far(part, r - 1)

        @pl.when(r == 4)
        def _():
            for k in range(4):
                arrived_far(0, k)

        plane = plane_of(r - 1)
        for s in range(16):
            for part in range(3):
                wch[pl.ds(s * COLS, COLS), pl.ds(part * PART, PART)] = wb[
                    part, plane, s // 4, s % 4
                ]
        near = pl.ds(pl.multiple_of(plane * PLANE, HD), PLANE)
        far = pl.ds(pl.multiple_of(g * HALF + plane * PLANE, HD), PLANE)
        for b in range(2):
            projected = dot(att[b], wch[...], NTDOT)
            mixed = (
                hid[b, :, near].astype(jnp.float32) + gate[pl.ds(b, 1), far] * projected
            ).astype(jnp.bfloat16)
            rows = pl.ds(b * ROWS, ROWS)
            zacc[:, rows] += dot(ft[b, :, near], mixed, NTDOT)
            wide = mixed.astype(jnp.float32)
            square = wide * wide
            sacc[rows, :] += square[:, :128] + square[:, 128:256] + square[:, 256:]
        return carry

    lax.fori_loop(1, 5, project, 0)

    squares = jnp.sum(jnp.transpose(sacc[...]), axis=0, keepdims=True)
    for base in (32, 80):
        block = zacc[pl.ds(base, 8), :]
        pick = lax.broadcasted_iota(jnp.int32, block.shape, 0) == 1
        zacc[pl.ds(base, 8), :] = jnp.where(pick, squares, block)
    zsend = remote(zacc.at[pl.ds(48, 48)], zrecv, part_s.at[4], part_r.at[4], partner)
    zsend.start()
    zsend.wait_recv()
    velocity = []
    for b in range(2):
        cols = pl.ds(b * ROWS, ROWS)
        total = zacc[pl.ds(0, 40), cols] + zrecv[pl.ds(0, 40), cols]
        mean = total[32:33] * (1.0 / D)
        square = total[33:34] * (1.0 / D)
        velocity.append(
            (total[:32] - mean * consts[b, 0, :, 0:1])
            * lax.rsqrt(square - mean * mean + norm_eps)
            + consts[b, 1, :, 0:1]
        )
    out[...] = velocity[1] + guidance * (velocity[0] - velocity[1])

    zsend.wait_send()
    hid_out.wait_send()
    att_s.wait_send()
    for c in w1 + w2:
        c.wait_send()
    for c in range(NC):
        block = att.at[g, :, pl.ds(HALF + c * 2 * JC * HD, 2 * JC * HD)]
        remote(block, block, part_s.at[2 + c], part_r.at[2 + c], partner).wait_send()
        wait_bytes(recv.at[c, pl.ds(0, FRAMES - 1)], qs_sem.at[c])
        wait_bytes(osend.at[c, pl.ds(0, FRAMES - 1)], os_sem.at[c])

    def drain(r, carry):
        for part in range(3):
            for way in range(2):
                direct(part, r, way).wait_send()
                forward(part, r, way).wait_send()
        return carry

    lax.fori_loop(0, 4, drain, 0)


def per_device(
    head_labels,
    queries,
    key_heads,
    value_heads,
    hidden_state,
    gate_scale,
    out_weight,
    final_scale,
    final_shift,
    final_weight,
    latent,
):
    anyspace = pl.BlockSpec(memory_space=pl.ANY)
    vmem = pl.BlockSpec(memory_space=pltpu.VMEM)
    smem = pl.BlockSpec(memory_space=pltpu.SMEM)
    bf16, f32 = jnp.bfloat16, jnp.float32
    dma = pltpu.SemaphoreType.DMA
    guided = pl.pallas_call(
        kernel,
        out_shape=jax.ShapeDtypeStruct((OUT_CH // 2, ROWS), f32),
        in_specs=[smem] + [anyspace] * 5 + [vmem] * 4,
        out_specs=vmem,
        scratch_shapes=[
            pltpu.VMEM((H, ROWS, HD), bf16),
            pltpu.VMEM((H, ROWS, HD), bf16),
            pltpu.VMEM((H, ROWS, HD), bf16),
            pltpu.VMEM((NC, FRAMES // 2, 2, QROWS, HD), bf16),
            pltpu.VMEM((NC, FRAMES, QROWS, HD), bf16),
            pltpu.VMEM((NC, FRAMES, OROWS, HD), bf16),
            pltpu.VMEM((NC, FRAMES // 2, 2, OROWS, HD), bf16),
            pltpu.VMEM((2, ROWS, D), bf16),
            pltpu.VMEM((H, COLS, HD), bf16),
            pltpu.VMEM((3, 4, 4, 4, COLS, PART), bf16),
            pltpu.VMEM((PLANE, D), bf16),
            pltpu.VMEM((2, ROWS, HALF), bf16),
            pltpu.VMEM((3, FRAMES * GP, HD), f32),
            pltpu.VMEM((FRAMES * GP, HD), f32),
            pltpu.VMEM((2, 96, HALF), bf16),
            pltpu.VMEM((2, 2, 32, HD), f32),
            pltpu.VMEM((96, 2 * ROWS), f32),
            pltpu.VMEM((2 * ROWS, HD), f32),
            pltpu.VMEM((48, 2 * ROWS), f32),
            dma((5,)), dma((2 * NC,)),
            dma((NC,)), dma((NC,)), dma((NC,)), dma((NC,)),
            dma((9,)), dma((3,)), dma((9,)), dma((3,)),
            dma((3, 4, 4)), dma((3, 4, 4)),
            dma((5,)), dma((5,)),
        ],
        compiler_params=pltpu.CompilerParams(
            collective_id=0, has_side_effects=True, vmem_limit_bytes=62 * 2**20
        ),
        cost_estimate=pl.CostEstimate(
            flops=16 * 10**9, bytes_accessed=20 * 10**6, transcendentals=4 * 10**6
        ),
        name="guided_layer",
    )(
        order_of(head_labels), queries, key_heads, value_heads, hidden_state,
        out_weight.T, final_weight.T, gate_scale, final_scale, final_shift,
    )
    return (latent.T - euler_step * guided).T


def solution(mesh):
    placed = (
        P(),
        P("guide", "frame", None),
        P("guide", "frame", None),
        P("guide", "frame", None),
        P("guide", "frame", None),
        P(),
        P(None, ("guide", "frame")),
        P(),
        P(),
        P(),
        P("frame", "guide"),
    )
    return jax.shard_map(
        per_device, mesh=mesh, in_specs=placed, out_specs=P("frame", "guide"), check_vma=False
    )
```

```python
import math

import jax
import jax.numpy as jnp
from jax import lax
from jax.experimental import pallas as pl
from jax.experimental.pallas import tpu as pltpu
from jax.sharding import PartitionSpec as P

H = 24
HD = 128
OUT_CH = 64
NT = 12
D = 3072
ROWS = 512
FRAMES = 64
HALF = D // 2
COLS = 24
GP = 16
NC = 2
JC = 3
QROWS = 3 * JC * GP
OROWS = JC * GP
PART = 1024
PLANE = 16 * COLS
MESH = pl.DeviceIdType.MESH
NTDOT = (((1,), (1,)), ((), ()))
NNDOT = (((1,), (0,)), ((), ()))

guidance = 6.0
euler_step = 0.25
norm_eps = 1e-06
SCORE_SCALE = 1.0 / math.sqrt(HD)


def dot(a, b, dims):
    return lax.dot_general(a, b, dims, preferred_element_type=jnp.float32)


def lanes_of(head):
    return pl.ds(pl.multiple_of(head * HD, HD), HD)


def kernel(
    labels, q_hbm, k_hbm, v_hbm, hid_hbm, w_hbm, f_ref, gate, scale, shift, out,
    qv, kv, vv, send, recv, osend, orecv, att, wsrc, wb, wch, hid, tmp, otmp, ft, consts,
    zacc, sacc, zrecv,
    load_sem, own_sem, qs_sem, qr_sem, os_sem, or_sem, w1s, w1r, w2s, w2r, w3s, w3r,
    part_s, part_r, step_sem, order, perm,
):
    g = lax.axis_index("guide")
    f = lax.axis_index("frame")
    z, x, y = f // 16, (f // 4) % 4, f % 4
    partner = (1 - g, f)

    def at(zz, xx, yy):
        return (g, lax.rem(zz, 4) * 16 + lax.rem(xx, 4) * 4 + lax.rem(yy, 4))

    def frame_of(i):
        a, b, c = lax.rem(i, 4), lax.rem(lax.div(i, 4), 4), lax.div(i, 16)
        return lax.rem(z + a + c, 4) * 16 + lax.rem(x + a + b, 4) * 4 + lax.rem(y + a, 4)

    def remote(src, dst, ssem, rsem, dev):
        return pltpu.make_async_remote_copy(
            src_ref=src, dst_ref=dst, send_sem=ssem, recv_sem=rsem,
            device_id=dev, device_id_type=MESH,
        )

    def wait_bytes(ref, sem):
        pltpu.make_async_copy(ref, ref, sem).wait()

    own_half = pl.ds(pl.multiple_of(g * HALF, HALF), HALF)
    other_half = pl.ds(pl.multiple_of((1 - g) * HALF, HALF), HALF)

    bar = pltpu.get_barrier_semaphore()
    pl.semaphore_signal(bar, inc=1, device_id=partner, device_id_type=MESH)
    for k in range(1, 4):
        pl.semaphore_signal(bar, inc=1, device_id=at(z + k, x, y), device_id_type=MESH)

    def greet(i, carry):
        dev = at(z, x + lax.div(i, 4), y + lax.rem(i, 4))
        pl.semaphore_signal(bar, inc=1, device_id=dev, device_id_type=MESH)
        return carry

    lax.fori_loop(1, 16, greet, 0)

    def load_w(h, carry):
        pltpu.make_async_copy(w_hbm.at[:, lanes_of(h)], wsrc.at[h], load_sem.at[0]).start()
        return carry

    def load(h, carry):
        lanes = lanes_of(h)
        for t, (src, dst) in enumerate(((q_hbm, qv), (k_hbm, kv), (v_hbm, vv))):
            pltpu.make_async_copy(src.at[0, :, lanes], dst.at[h], load_sem.at[1 + t]).start()
        return carry

    lax.fori_loop(0, H, load_w, 0)
    lax.fori_loop(0, H, load, 0)
    hid_in = pltpu.make_async_copy(hid_hbm.at[0, :, own_half], hid.at[g], load_sem.at[4])
    hid_in.start()

    slots, ones = [], jnp.int32(0)
    for h in range(H):
        slots.append(jnp.where(labels[h] == 0, h - ones, NT + ones))
        ones = ones + labels[h]
    for j in range(H):
        found = jnp.int32(0)
        for h in range(j % NT, j % NT + NT + 1):
            if h < H:
                found = jnp.where(slots[h] == j, jnp.int32(h), found)
        order[j] = found

    wait_bytes(wsrc, load_sem.at[0])
    for part in range(3):
        def permute(i, carry, part=part):
            j = part * 8 + i
            h = order[j]
            wb[part, z, x, y, :, pl.ds(pl.multiple_of(i * HD, HD), HD)] = wsrc[h]
            return carry

        lax.fori_loop(0, 8, permute, 0)

    pl.semaphore_wait(bar, 19)

    w1 = []
    for part in range(3):
        for k, step in enumerate((1, 3, 2)):
            dev = (at(z, x, y + step), at(z, x + step, y), at(z + step, x, y))[part]
            block = wb.at[part, z, x, y]
            w1.append(remote(block, block, w1s.at[part * 3 + k], w1r.at[part], dev))
    for c in w1:
        c.start()

    for k in range(1, 4):
        pl.semaphore_signal(step_sem, inc=1, device_id=at(z + k, x, y), device_id_type=MESH)
    hid_out = remote(
        hid_hbm.at[0, :, other_half], hid.at[g], part_s.at[0], part_r.at[0], partner
    )
    hid_out.start()

    for t, ref in enumerate((qv, kv, vv)):
        wait_bytes(ref, load_sem.at[1 + t])

    def gather(c):
        def body(i, carry):
            hh, jj = lax.div(i, JC), lax.rem(i, JC)
            h = order[NT + c * 2 * JC + i]
            for t, ref in enumerate((qv, kv, vv)):
                rows = pl.ds(pl.multiple_of((t * JC + jj) * GP, GP), GP)
                send[c, :, hh, rows, :] = ref[h].reshape(FRAMES // 2, GP, HD)
            return carry

        lax.fori_loop(0, 2 * JC, body, 0)

    def post(c):
        def body(i, carry):
            d = frame_of(i)
            remote(
                send.at[c, lax.div(d, 2), lax.rem(d, 2)], recv.at[c, f],
                qs_sem.at[c], qr_sem.at[c], (g, d),
            ).start()
            return carry

        lax.fori_loop(1, FRAMES, body, 0)
        pltpu.make_async_copy(send.at[c, f // 2, f % 2], recv.at[c, f], own_sem.at[c]).start()

    def shards(part, step, keep):
        if part == 0:
            return wb.at[0, z, (x + step) % 4, keep]
        if part == 1:
            return wb.at[1, (z + step) % 4, keep, y]
        return wb.at[2, keep, x, (y + step) % 4]

    whole, first, last = pl.ds(0, 4), pl.ds(0, 2), pl.ds(2, 2)

    def second(part, step):
        return (at(z, x + step, y), at(z + step, x, y), at(z, x, y + step))[part]

    gather(0)

    gather(1)
    pl.semaphore_wait(step_sem, 3)
    post(0)
    post(1)
    w2 = []
    for part in range(3):
        wait_bytes(wb.at[part, 0, 0, pl.ds(0, 3)], w1r.at[part])
        ref = shards(part, 0, whole)
        for k, step in enumerate((1, 3, 2)):
            c = remote(ref, ref, w2s.at[part * 3 + k], w2r.at[part], second(part, step))
            c.start()
            w2.append(c)


    def softmax(blocks):
        tops = [jnp.max(v, axis=-1, keepdims=True) for v in blocks]
        expd = [jnp.exp((v - top) * SCORE_SCALE) for v, top in zip(blocks, tops)]
        shares = [1.0 / jnp.sum(v, axis=-1, keepdims=True) for v in expd]
        return [(v * share).astype(jnp.bfloat16) for v, share in zip(expd, shares)]

    def spatial(js, carry):
        h = order[js]
        keys, values = kv[h], vv[h]
        out_lanes = pl.ds(pl.multiple_of(js * HD, HD), HD)
        blocks = [pl.ds(rb * 128, 128) for rb in range(4)]
        weights = softmax([dot(qv[h, rows, :], keys, NTDOT) for rows in blocks])
        for rows, weight in zip(blocks, weights):
            att[g, rows, out_lanes] = dot(weight, values, NNDOT).astype(jnp.bfloat16)
        return carry

    lax.fori_loop(0, NT, spatial, 0)
    half_s = att.at[g, :, pl.ds(0, HALF)]
    att_s = remote(half_s, half_s, part_s.at[1], part_r.at[1], partner)
    att_s.start()

    row_id = lax.broadcasted_iota(jnp.int32, (16, HALF), 0)
    ones_row = jnp.where(row_id == 0, 1.0, 0.0).astype(jnp.bfloat16)
    for b in range(2):
        own_scale = 1.0 + scale[pl.ds(b, 1), own_half]
        for base, who in ((0, g), (48, 1 - g)):
            chans = pl.ds(pl.multiple_of(who * 32, 32), 32)
            ft[b, pl.ds(base, 32), :] = (
                f_ref[chans, own_half].astype(jnp.float32) * own_scale
            ).astype(jnp.bfloat16)
            ft[b, pl.ds(base + 32, 16), :] = ones_row
        chans = pl.ds(pl.multiple_of(g * 32, 32), 32)
        wide = f_ref[chans, :].astype(jnp.float32)
        scaled = (wide * (1.0 + scale[pl.ds(b, 1), :])).astype(jnp.bfloat16).astype(jnp.float32)
        consts[b, 0] = jnp.broadcast_to(jnp.sum(scaled, axis=1, keepdims=True), (32, HD))
        consts[b, 1] = jnp.broadcast_to(
            jnp.sum(wide * shift[pl.ds(b, 1), :], axis=1, keepdims=True), (32, HD)
        )
    zacc[...] = jnp.zeros_like(zacc)
    sacc[...] = jnp.zeros_like(sacc)

    def plane_of(r):
        return (z + jnp.where(r == 2, 3, jnp.where(r == 3, 2, r))) % 4

    def neighbour(part, step):
        return (at(z + step, x, y), at(z, x, y + step), at(z, x + step, y))[part]

    def piece(part, r, step, keep):
        if part == 0:
            return wb.at[0, (z + step) % 4, r, keep]
        if part == 1:
            return wb.at[1, plane_of(r), keep, (y + step) % 4]
        return wb.at[2, plane_of(r), (x + step) % 4, keep]

    def direct(part, r, way):
        ref = piece(part, r, 0, whole)
        return remote(
            ref, ref, w3s.at[part, r, way], w3r.at[part, r, way],
            neighbour(part, (1, 3)[way]),
        )

    def forward(part, r, way):
        ref = piece(part, r, (3, 1)[way], (first, last)[way])
        return remote(
            ref, ref, w3s.at[part, r, 2 + way], w3r.at[part, r, 2 + way],
            neighbour(part, (1, 3)[way]),
        )

    def arrived(part, r):
        for way in range(2):
            wait_bytes(piece(part, r, (3, 1)[way], whole), w3r.at[part, r, way])

    def arrived_far(part, r):
        for way in range(2):
            wait_bytes(piece(part, r, 2, (first, last)[way]), w3r.at[part, r, 2 + way])

    def post_direct(part, r):
        for way in range(2):
            direct(part, r, way).start()

    def pass_on(part, r):
        arrived(part, r)
        for way in range(2):
            forward(part, r, way).start()

    def swapped(n):
        r = lax.broadcasted_iota(jnp.int32, (n, n), 0)
        c = lax.broadcasted_iota(jnp.int32, (n, n), 1)
        return (lax.rem(r, GP) == lax.div(c, GP)) & (lax.div(r, GP) == lax.rem(c, GP))

    perm[...] = jnp.where(swapped(GP * GP), 1.0, 0.0).astype(jnp.bfloat16)
    row_pos = lax.rem(lax.div(lax.broadcasted_iota(jnp.int32, (128, 128), 0), GP), 2)
    col_pos = lax.rem(lax.div(lax.broadcasted_iota(jnp.int32, (128, 128), 1), GP), 2)
    same = row_pos == col_pos

    def swap(one, two):
        both = dot(perm[...], jnp.concatenate([one, two], axis=1), NNDOT).astype(jnp.bfloat16)
        return both[:, :HD], both[:, HD:]

    def arrive(c):
        wait_bytes(recv.at[c, pl.ds(0, FRAMES - 1)], qr_sem.at[c])
        pltpu.make_async_copy(send.at[c, f // 2, f % 2], recv.at[c, f], own_sem.at[c]).wait()

    def attend(c):
        def temporal(jj, carry):
            def block(t, fb):
                rows = pl.ds(pl.multiple_of((t * JC + jj) * GP, GP), GP)
                return recv[c, pl.ds(fb * GP, GP), rows, :].reshape(GP * GP, HD)

            for one, two in [((0, fb), (1, fb)) for fb in range(4)] + [
                ((2, 0), (2, 1)), ((2, 2), (2, 3))
            ]:
                for (t, fb), val in zip((one, two), swap(block(*one), block(*two))):
                    tmp[t, fb] = val.reshape(GP, GP, HD)

            def pair_of(t, pair):
                return tmp[t, :, pl.ds(2 * pair, 2), :, :].reshape(128, HD)

            pairs = range(GP // 2)
            weights = softmax(
                [
                    jnp.where(same, dot(pair_of(0, pair), pair_of(1, pair), NTDOT), -1e30)
                    for pair in pairs
                ]
            )
            for pair, weight in zip(pairs, weights):
                result = dot(weight, pair_of(2, pair), NNDOT).astype(jnp.bfloat16)
                otmp[:, pl.ds(2 * pair, 2), :, :] = result.reshape(4, 2, GP, HD)
            rows = pl.ds(pl.multiple_of(jj * GP, GP), GP)
            for fb in (0, 2):
                pieces = swap(
                    otmp[fb].reshape(GP * GP, HD), otmp[fb + 1].reshape(GP * GP, HD)
                )
                for k in range(2):
                    osend[c, pl.ds((fb + k) * GP, GP), rows, :] = pieces[k].reshape(GP, GP, HD)
            return carry

        lax.fori_loop(0, JC, temporal, 0)

        def reply(i, carry):
            d = frame_of(i)
            remote(
                osend.at[c, d], orecv.at[c, f // 2, f % 2], os_sem.at[c], or_sem.at[c], (g, d)
            ).start()
            return carry

        lax.fori_loop(1, FRAMES, reply, 0)
        pltpu.make_async_copy(
            osend.at[c, f], orecv.at[c, f // 2, f % 2], own_sem.at[NC + c]
        ).start()

    def temporal_block(c):
        block = att.at[g, :, pl.ds(HALF + c * 2 * JC * HD, 2 * JC * HD)]
        return remote(block, block, part_s.at[2 + c], part_r.at[2 + c], partner)

    def collect(c):
        wait_bytes(osend.at[c, pl.ds(0, FRAMES - 1)], or_sem.at[c])
        pltpu.make_async_copy(
            osend.at[c, f], orecv.at[c, f // 2, f % 2], own_sem.at[NC + c]
        ).wait()
        for i in range(2 * JC):
            hh, jj = i // JC, i % JC
            lanes = pl.ds(HALF + (c * 2 * JC + i) * HD, HD)
            att[g, :, lanes] = orecv[c, :, hh, pl.ds(jj * GP, GP), :].reshape(ROWS, HD)
        temporal_block(c).start()

    arrive(0)
    attend(0)
    arrive(1)
    attend(1)
    for part in range(3):
        wait_bytes(wb.at[part, 0, pl.ds(0, 3)], w2r.at[part])
    post_direct(0, 0)
    post_direct(1, 0)
    post_direct(2, 0)
    post_direct(0, 1)
    post_direct(1, 1)
    post_direct(2, 1)
    collect(0)
    post_direct(0, 2)
    post_direct(1, 2)
    post_direct(2, 2)
    post_direct(0, 3)
    collect(1)
    pass_on(0, 0)
    pass_on(1, 0)
    pass_on(2, 0)
    post_direct(1, 3)
    post_direct(2, 3)
    pass_on(0, 1)
    pass_on(1, 1)
    pass_on(2, 1)
    hid_in.wait()
    hid_out.wait_recv()
    att_s.wait_recv()
    for c in range(NC):
        temporal_block(c).wait_recv()

    def project(r, carry):
        @pl.when((r == 2) | (r == 3))
        def _():
            for part in (1, 2):
                pass_on(part, r)

        @pl.when(r == 2)
        def _():
            for k in range(2, 4):
                pass_on(0, k)

        for part in (1, 2):
            arrived_far(part, r - 1)

        @pl.when(r == 4)
        def _():
            for k in range(4):
                arrived_far(0, k)

        plane = plane_of(r - 1)
        for s in range(16):
            for part in range(3):
                wch[pl.ds(s * COLS, COLS), pl.ds(part * PART, PART)] = wb[
                    part, plane, s // 4, s % 4
                ]
        near = pl.ds(pl.multiple_of(plane * PLANE, HD), PLANE)
        far = pl.ds(pl.multiple_of(g * HALF + plane * PLANE, HD), PLANE)
        for b in range(2):
            projected = dot(att[b], wch[...], NTDOT)
            mixed = (
                hid[b, :, near].astype(jnp.float32) + gate[pl.ds(b, 1), far] * projected
            ).astype(jnp.bfloat16)
            rows = pl.ds(b * ROWS, ROWS)
            zacc[:, rows] += dot(ft[b, :, near], mixed, NTDOT)
            wide = mixed.astype(jnp.float32)
            square = wide * wide
            sacc[rows, :] += square[:, :128] + square[:, 128:256] + square[:, 256:]
        return carry

    lax.fori_loop(1, 5, project, 0)

    squares = jnp.sum(jnp.transpose(sacc[...]), axis=0, keepdims=True)
    for base in (32, 80):
        block = zacc[pl.ds(base, 8), :]
        pick = lax.broadcasted_iota(jnp.int32, block.shape, 0) == 1
        zacc[pl.ds(base, 8), :] = jnp.where(pick, squares, block)
    zsend = remote(zacc.at[pl.ds(48, 48)], zrecv, part_s.at[4], part_r.at[4], partner)
    zsend.start()
    zsend.wait_recv()
    velocity = []
    for b in range(2):
        cols = pl.ds(b * ROWS, ROWS)
        total = zacc[pl.ds(0, 40), cols] + zrecv[pl.ds(0, 40), cols]
        mean = total[32:33] * (1.0 / D)
        square = total[33:34] * (1.0 / D)
        velocity.append(
            (total[:32] - mean * consts[b, 0, :, 0:1])
            * lax.rsqrt(square - mean * mean + norm_eps)
            + consts[b, 1, :, 0:1]
        )
    out[...] = velocity[1] + guidance * (velocity[0] - velocity[1])

    zsend.wait_send()
    hid_out.wait_send()
    att_s.wait_send()
    for c in w1 + w2:
        c.wait_send()
    for c in range(NC):
        temporal_block(c).wait_send()
        wait_bytes(recv.at[c, pl.ds(0, FRAMES - 1)], qs_sem.at[c])
        wait_bytes(osend.at[c, pl.ds(0, FRAMES - 1)], os_sem.at[c])

    def drain(r, carry):
        for part in range(3):
            for way in range(2):
                direct(part, r, way).wait_send()
                forward(part, r, way).wait_send()
        return carry

    lax.fori_loop(0, 4, drain, 0)


def per_device(
    head_labels,
    queries,
    key_heads,
    value_heads,
    hidden_state,
    gate_scale,
    out_weight,
    final_scale,
    final_shift,
    final_weight,
    latent,
):
    anyspace = pl.BlockSpec(memory_space=pl.ANY)
    vmem = pl.BlockSpec(memory_space=pltpu.VMEM)
    smem = pl.BlockSpec(memory_space=pltpu.SMEM)
    bf16, f32 = jnp.bfloat16, jnp.float32
    dma = pltpu.SemaphoreType.DMA
    guided = pl.pallas_call(
        kernel,
        out_shape=jax.ShapeDtypeStruct((OUT_CH // 2, ROWS), f32),
        in_specs=[smem] + [anyspace] * 5 + [vmem] * 4,
        out_specs=vmem,
        scratch_shapes=[
            pltpu.VMEM((H, ROWS, HD), bf16),
            pltpu.VMEM((H, ROWS, HD), bf16),
            pltpu.VMEM((H, ROWS, HD), bf16),
            pltpu.VMEM((NC, FRAMES // 2, 2, QROWS, HD), bf16),
            pltpu.VMEM((NC, FRAMES, QROWS, HD), bf16),
            pltpu.VMEM((NC, FRAMES, OROWS, HD), bf16),
            pltpu.VMEM((NC, FRAMES // 2, 2, OROWS, HD), bf16),
            pltpu.VMEM((2, ROWS, D), bf16),
            pltpu.VMEM((H, COLS, HD), bf16),
            pltpu.VMEM((3, 4, 4, 4, COLS, PART), bf16),
            pltpu.VMEM((PLANE, D), bf16),
            pltpu.VMEM((2, ROWS, HALF), bf16),
            pltpu.VMEM((3, 4, GP, GP, HD), bf16),
            pltpu.VMEM((4, GP, GP, HD), bf16),
            pltpu.VMEM((2, 96, HALF), bf16),
            pltpu.VMEM((2, 2, 32, HD), f32),
            pltpu.VMEM((96, 2 * ROWS), f32),
            pltpu.VMEM((2 * ROWS, HD), f32),
            pltpu.VMEM((48, 2 * ROWS), f32),
            dma((5,)), dma((2 * NC,)),
            dma((NC,)), dma((NC,)), dma((NC,)), dma((NC,)),
            dma((9,)), dma((3,)), dma((9,)), dma((3,)),
            dma((3, 4, 4)), dma((3, 4, 4)),
            dma((5,)), dma((5,)),
            pltpu.SemaphoreType.REGULAR,
            pltpu.SMEM((H,), jnp.int32),
            pltpu.VMEM((GP * GP, GP * GP), bf16),
        ],
        compiler_params=pltpu.CompilerParams(
            collective_id=0, has_side_effects=True, vmem_limit_bytes=62 * 2**20
        ),
        cost_estimate=pl.CostEstimate(
            flops=16 * 10**9, bytes_accessed=20 * 10**6, transcendentals=4 * 10**6
        ),
        name="guided_layer",
    )(
        head_labels, queries, key_heads, value_heads, hidden_state,
        out_weight.T, final_weight.T, gate_scale, final_scale, final_shift,
    )
    return (latent.T - euler_step * guided).T


def solution(mesh):
    placed = (
        P(),
        P("guide", "frame", None),
        P("guide", "frame", None),
        P("guide", "frame", None),
        P("guide", "frame", None),
        P(),
        P(None, ("guide", "frame")),
        P(),
        P(),
        P(),
        P("frame", "guide"),
    )
    return jax.shard_map(
        per_device, mesh=mesh, in_specs=placed, out_specs=P("frame", "guide"), check_vma=False
    )
```

```python
import math

import jax
import jax.numpy as jnp
from jax import lax
from jax.experimental import pallas as pl
from jax.experimental.pallas import tpu as pltpu
from jax.sharding import PartitionSpec as P

H = 24
HD = 128
OUT_CH = 64
NT = 12
D = 3072
ROWS = 512
FRAMES = 64
HALF = D // 2
COLS = 24
GP = 16
NC = 2
JC = 3
QROWS = 3 * JC * GP
OROWS = JC * GP
PART = 1024
PLANE = 16 * COLS
MESH = pl.DeviceIdType.MESH
NTDOT = (((1,), (1,)), ((), ()))
NNDOT = (((1,), (0,)), ((), ()))

guidance = 6.0
euler_step = 0.25
norm_eps = 1e-06
SCORE_SCALE = 1.0 / math.sqrt(HD)


def dot(a, b, dims):
    return lax.dot_general(a, b, dims, preferred_element_type=jnp.float32)


def lanes_of(head):
    return pl.ds(pl.multiple_of(head * HD, HD), HD)


def kernel(
    labels, q_hbm, k_hbm, v_hbm, hid_hbm, w_hbm, f_ref, gate, scale, shift, out,
    qv, kv, vv, send, recv, osend, orecv, att, wsrc, wb, wch, hid, tmp, otmp, ft, consts,
    zacc, sacc, zrecv,
    load_sem, own_sem, qs_sem, qr_sem, os_sem, or_sem, w1s, w1r, w2s, w2r, w3s, w3r,
    part_s, part_r, step_sem, order, perm,
):
    g = lax.axis_index("guide")
    f = lax.axis_index("frame")
    z, x, y = f // 16, (f // 4) % 4, f % 4
    partner = (1 - g, f)

    def at(zz, xx, yy):
        return (g, lax.rem(zz, 4) * 16 + lax.rem(xx, 4) * 4 + lax.rem(yy, 4))

    def frame_of(i):
        a, b, c = lax.rem(i, 4), lax.rem(lax.div(i, 4), 4), lax.div(i, 16)
        return lax.rem(z + a + c, 4) * 16 + lax.rem(x + a + b, 4) * 4 + lax.rem(y + a, 4)

    def remote(src, dst, ssem, rsem, dev):
        return pltpu.make_async_remote_copy(
            src_ref=src, dst_ref=dst, send_sem=ssem, recv_sem=rsem,
            device_id=dev, device_id_type=MESH,
        )

    def wait_bytes(ref, sem):
        pltpu.make_async_copy(ref, ref, sem).wait()

    own_half = pl.ds(pl.multiple_of(g * HALF, HALF), HALF)
    other_half = pl.ds(pl.multiple_of((1 - g) * HALF, HALF), HALF)

    bar = pltpu.get_barrier_semaphore()
    pl.semaphore_signal(bar, inc=1, device_id=partner, device_id_type=MESH)
    for k in range(1, 4):
        pl.semaphore_signal(bar, inc=1, device_id=at(z + k, x, y), device_id_type=MESH)

    def greet(i, carry):
        dev = at(z, x + lax.div(i, 4), y + lax.rem(i, 4))
        pl.semaphore_signal(bar, inc=1, device_id=dev, device_id_type=MESH)
        return carry

    lax.fori_loop(1, 16, greet, 0)

    def load_w(h, carry):
        pltpu.make_async_copy(w_hbm.at[:, lanes_of(h)], wsrc.at[h], load_sem.at[0]).start()
        return carry

    def load(h, carry):
        lanes = lanes_of(h)
        for t, (src, dst) in enumerate(((q_hbm, qv), (k_hbm, kv), (v_hbm, vv))):
            pltpu.make_async_copy(src.at[0, :, lanes], dst.at[h], load_sem.at[1 + t]).start()
        return carry

    lax.fori_loop(0, H, load_w, 0)
    lax.fori_loop(0, H, load, 0)
    hid_in = pltpu.make_async_copy(hid_hbm.at[0, :, own_half], hid.at[g], load_sem.at[4])
    hid_in.start()

    slots, ones = [], jnp.int32(0)
    for h in range(H):
        slots.append(jnp.where(labels[h] == 0, h - ones, NT + ones))
        ones = ones + labels[h]
    for j in range(H):
        found = jnp.int32(0)
        for h in range(j % NT, j % NT + NT + 1):
            if h < H:
                found = jnp.where(slots[h] == j, jnp.int32(h), found)
        order[j] = found

    wait_bytes(wsrc, load_sem.at[0])
    for part in range(3):
        def permute(i, carry, part=part):
            j = part * 8 + i
            h = order[j]
            wb[part, z, x, y, :, pl.ds(pl.multiple_of(i * HD, HD), HD)] = wsrc[h]
            return carry

        lax.fori_loop(0, 8, permute, 0)

    pl.semaphore_wait(bar, 19)

    w1 = []
    for part in range(3):
        for k, step in enumerate((1, 3, 2)):
            dev = (at(z, x, y + step), at(z, x + step, y), at(z + step, x, y))[part]
            block = wb.at[part, z, x, y]
            w1.append(remote(block, block, w1s.at[part * 3 + k], w1r.at[part], dev))
    for c in w1:
        c.start()

    for k in range(1, 4):
        pl.semaphore_signal(step_sem, inc=1, device_id=at(z + k, x, y), device_id_type=MESH)
    hid_out = remote(
        hid_hbm.at[0, :, other_half], hid.at[g], part_s.at[0], part_r.at[0], partner
    )
    hid_out.start()

    for t, ref in enumerate((qv, kv, vv)):
        wait_bytes(ref, load_sem.at[1 + t])

    def gather(c):
        def body(i, carry):
            hh, jj = lax.div(i, JC), lax.rem(i, JC)
            h = order[NT + c * 2 * JC + i]
            for t, ref in enumerate((qv, kv, vv)):
                rows = pl.ds(pl.multiple_of((t * JC + jj) * GP, GP), GP)
                send[c, :, hh, rows, :] = ref[h].reshape(FRAMES // 2, GP, HD)
            return carry

        lax.fori_loop(0, 2 * JC, body, 0)

    def post(c):
        def body(i, carry):
            d = frame_of(i)
            remote(
                send.at[c, lax.div(d, 2), lax.rem(d, 2)], recv.at[c, f],
                qs_sem.at[c], qr_sem.at[c], (g, d),
            ).start()
            return carry

        lax.fori_loop(1, FRAMES, body, 0)
        pltpu.make_async_copy(send.at[c, f // 2, f % 2], recv.at[c, f], own_sem.at[c]).start()

    def shards(part, step, keep):
        if part == 0:
            return wb.at[0, z, (x + step) % 4, keep]
        if part == 1:
            return wb.at[1, (z + step) % 4, keep, y]
        return wb.at[2, keep, x, (y + step) % 4]

    whole, first, last = pl.ds(0, 4), pl.ds(0, 2), pl.ds(2, 2)

    def second(part, step):
        return (at(z, x + step, y), at(z + step, x, y), at(z, x, y + step))[part]

    gather(0)

    gather(1)
    pl.semaphore_wait(step_sem, 3)
    post(0)
    w2 = []
    for part in range(3):
        wait_bytes(wb.at[part, 0, 0, pl.ds(0, 3)], w1r.at[part])
        ref = shards(part, 0, whole)
        for k, step in enumerate((1, 3, 2)):
            c = remote(ref, ref, w2s.at[part * 3 + k], w2r.at[part], second(part, step))
            c.start()
            w2.append(c)

    post(1)

    def softmax(blocks):
        tops = [jnp.max(v, axis=-1, keepdims=True) for v in blocks]
        expd = [jnp.exp((v - top) * SCORE_SCALE) for v, top in zip(blocks, tops)]
        shares = [1.0 / jnp.sum(v, axis=-1, keepdims=True) for v in expd]
        return [(v * share).astype(jnp.bfloat16) for v, share in zip(expd, shares)]

    def spatial(js, carry):
        h = order[js]
        keys, values = kv[h], vv[h]
        out_lanes = pl.ds(pl.multiple_of(js * HD, HD), HD)
        blocks = [pl.ds(rb * 128, 128) for rb in range(4)]
        weights = softmax([dot(qv[h, rows, :], keys, NTDOT) for rows in blocks])
        for rows, weight in zip(blocks, weights):
            att[g, rows, out_lanes] = dot(weight, values, NNDOT).astype(jnp.bfloat16)
        return carry

    lax.fori_loop(0, NT, spatial, 0)
    half_s = att.at[g, :, pl.ds(0, HALF)]
    att_s = remote(half_s, half_s, part_s.at[1], part_r.at[1], partner)
    att_s.start()

    row_id = lax.broadcasted_iota(jnp.int32, (16, HALF), 0)
    ones_row = jnp.where(row_id == 0, 1.0, 0.0).astype(jnp.bfloat16)
    for b in range(2):
        own_scale = 1.0 + scale[pl.ds(b, 1), own_half]
        for base, who in ((0, g), (48, 1 - g)):
            chans = pl.ds(pl.multiple_of(who * 32, 32), 32)
            ft[b, pl.ds(base, 32), :] = (
                f_ref[chans, own_half].astype(jnp.float32) * own_scale
            ).astype(jnp.bfloat16)
            ft[b, pl.ds(base + 32, 16), :] = ones_row
        chans = pl.ds(pl.multiple_of(g * 32, 32), 32)
        wide = f_ref[chans, :].astype(jnp.float32)
        scaled = (wide * (1.0 + scale[pl.ds(b, 1), :])).astype(jnp.bfloat16).astype(jnp.float32)
        consts[b, 0] = jnp.broadcast_to(jnp.sum(scaled, axis=1, keepdims=True), (32, HD))
        consts[b, 1] = jnp.broadcast_to(
            jnp.sum(wide * shift[pl.ds(b, 1), :], axis=1, keepdims=True), (32, HD)
        )
    zacc[...] = jnp.zeros_like(zacc)
    sacc[...] = jnp.zeros_like(sacc)

    def plane_of(r):
        return (z + jnp.where(r == 2, 3, jnp.where(r == 3, 2, r))) % 4

    def neighbour(part, step):
        return (at(z + step, x, y), at(z, x, y + step), at(z, x + step, y))[part]

    def piece(part, r, step, keep):
        if part == 0:
            return wb.at[0, (z + step) % 4, r, keep]
        if part == 1:
            return wb.at[1, plane_of(r), keep, (y + step) % 4]
        return wb.at[2, plane_of(r), (x + step) % 4, keep]

    def direct(part, r, way):
        ref = piece(part, r, 0, whole)
        return remote(
            ref, ref, w3s.at[part, r, way], w3r.at[part, r, way],
            neighbour(part, (1, 3)[way]),
        )

    def forward(part, r, way):
        ref = piece(part, r, (3, 1)[way], (first, last)[way])
        return remote(
            ref, ref, w3s.at[part, r, 2 + way], w3r.at[part, r, 2 + way],
            neighbour(part, (1, 3)[way]),
        )

    def arrived(part, r):
        for way in range(2):
            wait_bytes(piece(part, r, (3, 1)[way], whole), w3r.at[part, r, way])

    def arrived_far(part, r):
        for way in range(2):
            wait_bytes(piece(part, r, 2, (first, last)[way]), w3r.at[part, r, 2 + way])

    def post_direct(part, r):
        for way in range(2):
            direct(part, r, way).start()

    def pass_on(part, r):
        arrived(part, r)
        for way in range(2):
            forward(part, r, way).start()

    def swapped(n):
        r = lax.broadcasted_iota(jnp.int32, (n, n), 0)
        c = lax.broadcasted_iota(jnp.int32, (n, n), 1)
        return (lax.rem(r, GP) == lax.div(c, GP)) & (lax.div(r, GP) == lax.rem(c, GP))

    perm[...] = jnp.where(swapped(GP * GP), 1.0, 0.0).astype(jnp.bfloat16)
    row_pos = lax.rem(lax.div(lax.broadcasted_iota(jnp.int32, (128, 128), 0), GP), 2)
    col_pos = lax.rem(lax.div(lax.broadcasted_iota(jnp.int32, (128, 128), 1), GP), 2)
    same = row_pos == col_pos

    def swap(one, two):
        both = dot(perm[...], jnp.concatenate([one, two], axis=1), NNDOT).astype(jnp.bfloat16)
        return both[:, :HD], both[:, HD:]

    def arrive(c):
        wait_bytes(recv.at[c, pl.ds(0, FRAMES - 1)], qr_sem.at[c])
        pltpu.make_async_copy(send.at[c, f // 2, f % 2], recv.at[c, f], own_sem.at[c]).wait()

    def attend(c):
        def temporal(jj, carry):
            def block(t, fb):
                rows = pl.ds(pl.multiple_of((t * JC + jj) * GP, GP), GP)
                return recv[c, pl.ds(fb * GP, GP), rows, :].reshape(GP * GP, HD)

            for one, two in [((0, fb), (1, fb)) for fb in range(4)] + [
                ((2, 0), (2, 1)), ((2, 2), (2, 3))
            ]:
                for (t, fb), val in zip((one, two), swap(block(*one), block(*two))):
                    tmp[t, fb] = val.reshape(GP, GP, HD)

            def pair_of(t, pair):
                return tmp[t, :, pl.ds(2 * pair, 2), :, :].reshape(128, HD)

            pairs = range(GP // 2)
            weights = softmax(
                [
                    jnp.where(same, dot(pair_of(0, pair), pair_of(1, pair), NTDOT), -1e30)
                    for pair in pairs
                ]
            )
            for pair, weight in zip(pairs, weights):
                result = dot(weight, pair_of(2, pair), NNDOT).astype(jnp.bfloat16)
                otmp[:, pl.ds(2 * pair, 2), :, :] = result.reshape(4, 2, GP, HD)
            rows = pl.ds(pl.multiple_of(jj * GP, GP), GP)
            for fb in (0, 2):
                pieces = swap(
                    otmp[fb].reshape(GP * GP, HD), otmp[fb + 1].reshape(GP * GP, HD)
                )
                for k in range(2):
                    osend[c, pl.ds((fb + k) * GP, GP), rows, :] = pieces[k].reshape(GP, GP, HD)
            return carry

        lax.fori_loop(0, JC, temporal, 0)

        def reply(i, carry):
            d = frame_of(i)
            remote(
                osend.at[c, d], orecv.at[c, f // 2, f % 2], os_sem.at[c], or_sem.at[c], (g, d)
            ).start()
            return carry

        lax.fori_loop(1, FRAMES, reply, 0)
        pltpu.make_async_copy(
            osend.at[c, f], orecv.at[c, f // 2, f % 2], own_sem.at[NC + c]
        ).start()

    def temporal_block(c):
        block = att.at[g, :, pl.ds(HALF + c * 2 * JC * HD, 2 * JC * HD)]
        return remote(block, block, part_s.at[2 + c], part_r.at[2 + c], partner)

    def collect(c):
        wait_bytes(osend.at[c, pl.ds(0, FRAMES - 1)], or_sem.at[c])
        pltpu.make_async_copy(
            osend.at[c, f], orecv.at[c, f // 2, f % 2], own_sem.at[NC + c]
        ).wait()
        for i in range(2 * JC):
            hh, jj = i // JC, i % JC
            lanes = pl.ds(HALF + (c * 2 * JC + i) * HD, HD)
            att[g, :, lanes] = orecv[c, :, hh, pl.ds(jj * GP, GP), :].reshape(ROWS, HD)
        temporal_block(c).start()

    arrive(0)
    attend(0)
    arrive(1)
    for part in range(3):
        wait_bytes(wb.at[part, 0, pl.ds(0, 3)], w2r.at[part])
    post_direct(0, 0)
    post_direct(1, 0)
    post_direct(2, 0)
    attend(1)
    post_direct(0, 1)
    post_direct(1, 1)
    post_direct(2, 1)
    pass_on(0, 0)
    pass_on(1, 0)
    pass_on(2, 0)
    post_direct(0, 2)
    post_direct(1, 2)
    post_direct(2, 2)
    post_direct(0, 3)
    collect(0)
    pass_on(0, 1)
    pass_on(1, 1)
    pass_on(2, 1)
    post_direct(1, 3)
    post_direct(2, 3)
    collect(1)
    hid_in.wait()
    hid_out.wait_recv()
    att_s.wait_recv()
    for c in range(NC):
        temporal_block(c).wait_recv()

    def project(r, carry):
        @pl.when((r == 2) | (r == 3))
        def _():
            for part in (1, 2):
                pass_on(part, r)

        @pl.when(r == 2)
        def _():
            for k in range(2, 4):
                pass_on(0, k)

        for part in (1, 2):
            arrived_far(part, r - 1)

        @pl.when(r == 4)
        def _():
            for k in range(4):
                arrived_far(0, k)

        plane = plane_of(r - 1)
        for s in range(16):
            for part in range(3):
                wch[pl.ds(s * COLS, COLS), pl.ds(part * PART, PART)] = wb[
                    part, plane, s // 4, s % 4
                ]
        near = pl.ds(pl.multiple_of(plane * PLANE, HD), PLANE)
        far = pl.ds(pl.multiple_of(g * HALF + plane * PLANE, HD), PLANE)
        for b in range(2):
            projected = dot(att[b], wch[...], NTDOT)
            mixed = (
                hid[b, :, near].astype(jnp.float32) + gate[pl.ds(b, 1), far] * projected
            ).astype(jnp.bfloat16)
            rows = pl.ds(b * ROWS, ROWS)
            zacc[:, rows] += dot(ft[b, :, near], mixed, NTDOT)
            wide = mixed.astype(jnp.float32)
            square = wide * wide
            sacc[rows, :] += square[:, :128] + square[:, 128:256] + square[:, 256:]
        return carry

    lax.fori_loop(1, 5, project, 0)

    squares = jnp.sum(jnp.transpose(sacc[...]), axis=0, keepdims=True)
    for base in (32, 80):
        block = zacc[pl.ds(base, 8), :]
        pick = lax.broadcasted_iota(jnp.int32, block.shape, 0) == 1
        zacc[pl.ds(base, 8), :] = jnp.where(pick, squares, block)
    zsend = remote(zacc.at[pl.ds(48, 48)], zrecv, part_s.at[4], part_r.at[4], partner)
    zsend.start()
    hid_out.wait_send()
    att_s.wait_send()
    for c in w1 + w2:
        c.wait_send()
    for c in range(NC):
        temporal_block(c).wait_send()
        wait_bytes(recv.at[c, pl.ds(0, FRAMES - 1)], qs_sem.at[c])
        wait_bytes(osend.at[c, pl.ds(0, FRAMES - 1)], os_sem.at[c])

    def drain(r, carry):
        for part in range(3):
            for way in range(2):
                direct(part, r, way).wait_send()
                forward(part, r, way).wait_send()
        return carry

    lax.fori_loop(0, 4, drain, 0)

    zsend.wait_recv()
    velocity = []
    for b in range(2):
        cols = pl.ds(b * ROWS, ROWS)
        total = zacc[pl.ds(0, 40), cols] + zrecv[pl.ds(0, 40), cols]
        mean = total[32:33] * (1.0 / D)
        square = total[33:34] * (1.0 / D)
        velocity.append(
            (total[:32] - mean * consts[b, 0, :, 0:1])
            * lax.rsqrt(square - mean * mean + norm_eps)
            + consts[b, 1, :, 0:1]
        )
    out[...] = velocity[1] + guidance * (velocity[0] - velocity[1])
    zsend.wait_send()


def per_device(
    head_labels,
    queries,
    key_heads,
    value_heads,
    hidden_state,
    gate_scale,
    out_weight,
    final_scale,
    final_shift,
    final_weight,
    latent,
):
    anyspace = pl.BlockSpec(memory_space=pl.ANY)
    vmem = pl.BlockSpec(memory_space=pltpu.VMEM)
    smem = pl.BlockSpec(memory_space=pltpu.SMEM)
    bf16, f32 = jnp.bfloat16, jnp.float32
    dma = pltpu.SemaphoreType.DMA
    guided = pl.pallas_call(
        kernel,
        out_shape=jax.ShapeDtypeStruct((OUT_CH // 2, ROWS), f32),
        in_specs=[smem] + [anyspace] * 5 + [vmem] * 4,
        out_specs=vmem,
        scratch_shapes=[
            pltpu.VMEM((H, ROWS, HD), bf16),
            pltpu.VMEM((H, ROWS, HD), bf16),
            pltpu.VMEM((H, ROWS, HD), bf16),
            pltpu.VMEM((NC, FRAMES // 2, 2, QROWS, HD), bf16),
            pltpu.VMEM((NC, FRAMES, QROWS, HD), bf16),
            pltpu.VMEM((NC, FRAMES, OROWS, HD), bf16),
            pltpu.VMEM((NC, FRAMES // 2, 2, OROWS, HD), bf16),
            pltpu.VMEM((2, ROWS, D), bf16),
            pltpu.VMEM((H, COLS, HD), bf16),
            pltpu.VMEM((3, 4, 4, 4, COLS, PART), bf16),
            pltpu.VMEM((PLANE, D), bf16),
            pltpu.VMEM((2, ROWS, HALF), bf16),
            pltpu.VMEM((3, 4, GP, GP, HD), bf16),
            pltpu.VMEM((4, GP, GP, HD), bf16),
            pltpu.VMEM((2, 96, HALF), bf16),
            pltpu.VMEM((2, 2, 32, HD), f32),
            pltpu.VMEM((96, 2 * ROWS), f32),
            pltpu.VMEM((2 * ROWS, HD), f32),
            pltpu.VMEM((48, 2 * ROWS), f32),
            dma((5,)), dma((2 * NC,)),
            dma((NC,)), dma((NC,)), dma((NC,)), dma((NC,)),
            dma((9,)), dma((3,)), dma((9,)), dma((3,)),
            dma((3, 4, 4)), dma((3, 4, 4)),
            dma((5,)), dma((5,)),
            pltpu.SemaphoreType.REGULAR,
            pltpu.SMEM((H,), jnp.int32),
            pltpu.VMEM((GP * GP, GP * GP), bf16),
        ],
        compiler_params=pltpu.CompilerParams(
            collective_id=0, has_side_effects=True, vmem_limit_bytes=62 * 2**20
        ),
        cost_estimate=pl.CostEstimate(
            flops=16 * 10**9, bytes_accessed=20 * 10**6, transcendentals=4 * 10**6
        ),
        name="guided_layer",
    )(
        head_labels, queries, key_heads, value_heads, hidden_state,
        out_weight.T, final_weight.T, gate_scale, final_scale, final_shift,
    )
    return (latent.T - euler_step * guided).T


def solution(mesh):
    placed = (
        P(),
        P("guide", "frame", None),
        P("guide", "frame", None),
        P("guide", "frame", None),
        P("guide", "frame", None),
        P(),
        P(None, ("guide", "frame")),
        P(),
        P(),
        P(),
        P("frame", "guide"),
    )
    return jax.shard_map(
        per_device, mesh=mesh, in_specs=placed, out_specs=P("frame", "guide"), check_vma=False
    )
```

```python
import math

import jax
import jax.numpy as jnp
from jax import lax
from jax.experimental import pallas as pl
from jax.experimental.pallas import tpu as pltpu
from jax.sharding import PartitionSpec as P

H = 24
HD = 128
OUT_CH = 64
NT = 12
D = 3072
ROWS = 512
FRAMES = 64
HALF = D // 2
COLS = 24
GP = 16
NC = 2
JC = 3
QROWS = 3 * JC * GP
OROWS = JC * GP
PART = 1024
PLANE = 16 * COLS
MESH = pl.DeviceIdType.MESH
NTDOT = (((1,), (1,)), ((), ()))
NNDOT = (((1,), (0,)), ((), ()))

guidance = 6.0
euler_step = 0.25
norm_eps = 1e-06
SCORE_SCALE = 1.0 / math.sqrt(HD)


def dot(a, b, dims):
    return lax.dot_general(a, b, dims, preferred_element_type=jnp.float32)


def lanes_of(head):
    return pl.ds(pl.multiple_of(head * HD, HD), HD)


def kernel(
    labels, q_hbm, k_hbm, v_hbm, hid_hbm, w_hbm, f_ref, gate, scale, shift, out,
    qv, kv, vv, send, recv, osend, orecv, att, wsrc, wb, wch, hid, tmp, otmp, ft, consts,
    zacc, sacc, zrecv,
    load_sem, own_sem, qs_sem, qr_sem, os_sem, or_sem, w1s, w1r, w2s, w2r, w3s, w3r,
    part_s, part_r, step_sem, order, perm,
):
    g = lax.axis_index("guide")
    f = lax.axis_index("frame")
    z, x, y = f // 16, (f // 4) % 4, f % 4
    partner = (1 - g, f)

    def at(zz, xx, yy):
        return (g, lax.rem(zz, 4) * 16 + lax.rem(xx, 4) * 4 + lax.rem(yy, 4))

    def frame_of(i):
        a, b, c = lax.rem(i, 4), lax.rem(lax.div(i, 4), 4), lax.div(i, 16)
        return lax.rem(z + a + c, 4) * 16 + lax.rem(x + a + b, 4) * 4 + lax.rem(y + a, 4)

    def remote(src, dst, ssem, rsem, dev):
        return pltpu.make_async_remote_copy(
            src_ref=src, dst_ref=dst, send_sem=ssem, recv_sem=rsem,
            device_id=dev, device_id_type=MESH,
        )

    def wait_bytes(ref, sem):
        pltpu.make_async_copy(ref, ref, sem).wait()

    own_half = pl.ds(pl.multiple_of(g * HALF, HALF), HALF)
    other_half = pl.ds(pl.multiple_of((1 - g) * HALF, HALF), HALF)

    bar = pltpu.get_barrier_semaphore()
    pl.semaphore_signal(bar, inc=1, device_id=partner, device_id_type=MESH)
    for k in range(1, 4):
        pl.semaphore_signal(bar, inc=1, device_id=at(z + k, x, y), device_id_type=MESH)

    def greet(i, carry):
        dev = at(z, x + lax.div(i, 4), y + lax.rem(i, 4))
        pl.semaphore_signal(bar, inc=1, device_id=dev, device_id_type=MESH)
        return carry

    lax.fori_loop(1, 16, greet, 0)

    def load_w(h, carry):
        pltpu.make_async_copy(w_hbm.at[:, lanes_of(h)], wsrc.at[h], load_sem.at[0]).start()
        return carry

    def load(h, carry):
        lanes = lanes_of(h)
        for t, (src, dst) in enumerate(((q_hbm, qv), (k_hbm, kv), (v_hbm, vv))):
            pltpu.make_async_copy(src.at[0, :, lanes], dst.at[h], load_sem.at[1 + t]).start()
        return carry

    lax.fori_loop(0, H, load_w, 0)
    lax.fori_loop(0, H, load, 0)
    hid_in = pltpu.make_async_copy(hid_hbm.at[0, :, own_half], hid.at[g], load_sem.at[4])
    hid_in.start()

    slots, ones = [], jnp.int32(0)
    for h in range(H):
        slots.append(jnp.where(labels[h] == 0, h - ones, NT + ones))
        ones = ones + labels[h]
    for j in range(H):
        found = jnp.int32(0)
        for h in range(j % NT, j % NT + NT + 1):
            if h < H:
                found = jnp.where(slots[h] == j, jnp.int32(h), found)
        order[j] = found

    wait_bytes(wsrc, load_sem.at[0])
    for part in range(3):
        def permute(i, carry, part=part):
            j = part * 8 + i
            h = order[j]
            wb[part, z, x, y, :, pl.ds(pl.multiple_of(i * HD, HD), HD)] = wsrc[h]
            return carry

        lax.fori_loop(0, 8, permute, 0)

    pl.semaphore_wait(bar, 19)

    w1 = []
    for part in range(3):
        for k, step in enumerate((1, 3, 2)):
            dev = (at(z, x, y + step), at(z, x + step, y), at(z + step, x, y))[part]
            block = wb.at[part, z, x, y]
            w1.append(remote(block, block, w1s.at[part * 3 + k], w1r.at[part], dev))
    for c in w1:
        c.start()

    for k in range(1, 4):
        pl.semaphore_signal(step_sem, inc=1, device_id=at(z + k, x, y), device_id_type=MESH)
    hid_out = remote(
        hid_hbm.at[0, :, other_half], hid.at[g], part_s.at[0], part_r.at[0], partner
    )
    hid_out.start()

    for t, ref in enumerate((qv, kv, vv)):
        wait_bytes(ref, load_sem.at[1 + t])

    def gather(c):
        def body(i, carry):
            hh, jj = lax.div(i, JC), lax.rem(i, JC)
            h = order[NT + c * 2 * JC + i]
            for t, ref in enumerate((qv, kv, vv)):
                rows = pl.ds(pl.multiple_of((t * JC + jj) * GP, GP), GP)
                send[c, :, hh, rows, :] = ref[h].reshape(FRAMES // 2, GP, HD)
            return carry

        lax.fori_loop(0, 2 * JC, body, 0)

    def post(c):
        def body(i, carry):
            d = frame_of(i)
            remote(
                send.at[c, lax.div(d, 2), lax.rem(d, 2)], recv.at[c, f],
                qs_sem.at[c], qr_sem.at[c], (g, d),
            ).start()
            return carry

        lax.fori_loop(1, FRAMES, body, 0)
        pltpu.make_async_copy(send.at[c, f // 2, f % 2], recv.at[c, f], own_sem.at[c]).start()

    def shards(part, step, keep):
        if part == 0:
            return wb.at[0, z, (x + step) % 4, keep]
        if part == 1:
            return wb.at[1, (z + step) % 4, keep, y]
        return wb.at[2, keep, x, (y + step) % 4]

    whole, first, last = pl.ds(0, 4), pl.ds(0, 2), pl.ds(2, 2)

    def second(part, step):
        return (at(z, x + step, y), at(z + step, x, y), at(z, x, y + step))[part]

    gather(0)

    gather(1)
    pl.semaphore_wait(step_sem, 3)
    post(0)
    w2 = []
    for part in range(3):
        wait_bytes(wb.at[part, 0, 0, pl.ds(0, 3)], w1r.at[part])
        ref = shards(part, 0, whole)
        for k, step in enumerate((1, 3, 2)):
            c = remote(ref, ref, w2s.at[part * 3 + k], w2r.at[part], second(part, step))
            c.start()
            w2.append(c)

    post(1)

    def softmax(blocks):
        tops = [jnp.max(v, axis=-1, keepdims=True) for v in blocks]
        expd = [jnp.exp((v - top) * SCORE_SCALE) for v, top in zip(blocks, tops)]
        shares = [1.0 / jnp.sum(v, axis=-1, keepdims=True) for v in expd]
        return [(v * share).astype(jnp.bfloat16) for v, share in zip(expd, shares)]

    def spatial(js, carry):
        h = order[js]
        keys, values = kv[h], vv[h]
        out_lanes = pl.ds(pl.multiple_of(js * HD, HD), HD)
        blocks = [pl.ds(rb * 128, 128) for rb in range(4)]
        weights = softmax([dot(qv[h, rows, :], keys, NTDOT) for rows in blocks])
        for rows, weight in zip(blocks, weights):
            att[g, rows, out_lanes] = dot(weight, values, NNDOT).astype(jnp.bfloat16)
        return carry

    lax.fori_loop(0, NT, spatial, 0)
    half_s = att.at[g, :, pl.ds(0, HALF)]
    att_s = remote(half_s, half_s, part_s.at[1], part_r.at[1], partner)
    att_s.start()

    row_id = lax.broadcasted_iota(jnp.int32, (16, HALF), 0)
    ones_row = jnp.where(row_id == 0, 1.0, 0.0).astype(jnp.bfloat16)
    for b in range(2):
        own_scale = 1.0 + scale[pl.ds(b, 1), own_half]
        for base, who in ((0, g), (48, 1 - g)):
            chans = pl.ds(pl.multiple_of(who * 32, 32), 32)
            ft[b, pl.ds(base, 32), :] = (
                f_ref[chans, own_half].astype(jnp.float32) * own_scale
            ).astype(jnp.bfloat16)
            ft[b, pl.ds(base + 32, 16), :] = ones_row
        chans = pl.ds(pl.multiple_of(g * 32, 32), 32)
        wide = f_ref[chans, :].astype(jnp.float32)
        scaled = (wide * (1.0 + scale[pl.ds(b, 1), :])).astype(jnp.bfloat16).astype(jnp.float32)
        consts[b, 0] = jnp.broadcast_to(jnp.sum(scaled, axis=1, keepdims=True), (32, HD))
        consts[b, 1] = jnp.broadcast_to(
            jnp.sum(wide * shift[pl.ds(b, 1), :], axis=1, keepdims=True), (32, HD)
        )
    zacc[...] = jnp.zeros_like(zacc)
    sacc[...] = jnp.zeros_like(sacc)

    def plane_of(r):
        return (z + jnp.where(r == 2, 3, jnp.where(r == 3, 2, r))) % 4

    def neighbour(part, step):
        return (at(z + step, x, y), at(z, x, y + step), at(z, x + step, y))[part]

    def piece(part, r, step, keep):
        if part == 0:
            return wb.at[0, (z + step) % 4, r, keep]
        if part == 1:
            return wb.at[1, plane_of(r), keep, (y + step) % 4]
        return wb.at[2, plane_of(r), (x + step) % 4, keep]

    def direct(part, r, way):
        ref = piece(part, r, 0, whole)
        return remote(
            ref, ref, w3s.at[part, r, way], w3r.at[part, r, way],
            neighbour(part, (1, 3)[way]),
        )

    def forward(part, r, way):
        ref = piece(part, r, (3, 1)[way], (first, last)[way])
        return remote(
            ref, ref, w3s.at[part, r, 2 + way], w3r.at[part, r, 2 + way],
            neighbour(part, (1, 3)[way]),
        )

    def arrived(part, r):
        for way in range(2):
            wait_bytes(piece(part, r, (3, 1)[way], whole), w3r.at[part, r, way])

    def arrived_far(part, r):
        for way in range(2):
            wait_bytes(piece(part, r, 2, (first, last)[way]), w3r.at[part, r, 2 + way])

    def post_direct(part, r):
        for way in range(2):
            direct(part, r, way).start()

    def pass_on(part, r):
        arrived(part, r)
        for way in range(2):
            forward(part, r, way).start()

    def swapped(n):
        r = lax.broadcasted_iota(jnp.int32, (n, n), 0)
        c = lax.broadcasted_iota(jnp.int32, (n, n), 1)
        return (lax.rem(r, GP) == lax.div(c, GP)) & (lax.div(r, GP) == lax.rem(c, GP))

    perm[...] = jnp.where(swapped(GP * GP), 1.0, 0.0).astype(jnp.bfloat16)
    row_pos = lax.rem(lax.div(lax.broadcasted_iota(jnp.int32, (128, 128), 0), GP), 2)
    col_pos = lax.rem(lax.div(lax.broadcasted_iota(jnp.int32, (128, 128), 1), GP), 2)
    same = row_pos == col_pos

    def swap(one, two):
        both = dot(perm[...], jnp.concatenate([one, two], axis=1), NNDOT).astype(jnp.bfloat16)
        return both[:, :HD], both[:, HD:]

    def arrive(c):
        wait_bytes(recv.at[c, pl.ds(0, FRAMES - 1)], qr_sem.at[c])
        pltpu.make_async_copy(send.at[c, f // 2, f % 2], recv.at[c, f], own_sem.at[c]).wait()

    def attend(c):
        def temporal(jj, carry):
            def block(t, fb):
                rows = pl.ds(pl.multiple_of((t * JC + jj) * GP, GP), GP)
                return recv[c, pl.ds(fb * GP, GP), rows, :].reshape(GP * GP, HD)

            for one, two in [((0, fb), (1, fb)) for fb in range(4)] + [
                ((2, 0), (2, 1)), ((2, 2), (2, 3))
            ]:
                for (t, fb), val in zip((one, two), swap(block(*one), block(*two))):
                    tmp[t, fb] = val.reshape(GP, GP, HD)

            def pair_of(t, pair):
                return tmp[t, :, pl.ds(2 * pair, 2), :, :].reshape(128, HD)

            pairs = range(GP // 2)
            weights = softmax(
                [
                    jnp.where(same, dot(pair_of(0, pair), pair_of(1, pair), NTDOT), -1e30)
                    for pair in pairs
                ]
            )
            for pair, weight in zip(pairs, weights):
                result = dot(weight, pair_of(2, pair), NNDOT).astype(jnp.bfloat16)
                otmp[:, pl.ds(2 * pair, 2), :, :] = result.reshape(4, 2, GP, HD)
            rows = pl.ds(pl.multiple_of(jj * GP, GP), GP)
            for fb in (0, 2):
                pieces = swap(
                    otmp[fb].reshape(GP * GP, HD), otmp[fb + 1].reshape(GP * GP, HD)
                )
                for k in range(2):
                    osend[c, pl.ds((fb + k) * GP, GP), rows, :] = pieces[k].reshape(GP, GP, HD)
            return carry

        lax.fori_loop(0, JC, temporal, 0)

        def reply(i, carry):
            d = frame_of(i)
            remote(
                osend.at[c, d], orecv.at[c, f // 2, f % 2], os_sem.at[c], or_sem.at[c], (g, d)
            ).start()
            return carry

        lax.fori_loop(1, FRAMES, reply, 0)
        pltpu.make_async_copy(
            osend.at[c, f], orecv.at[c, f // 2, f % 2], own_sem.at[NC + c]
        ).start()

    def temporal_block(c):
        block = att.at[g, :, pl.ds(HALF + c * 2 * JC * HD, 2 * JC * HD)]
        return remote(block, block, part_s.at[2 + c], part_r.at[2 + c], partner)

    def collect(c):
        wait_bytes(osend.at[c, pl.ds(0, FRAMES - 1)], or_sem.at[c])
        pltpu.make_async_copy(
            osend.at[c, f], orecv.at[c, f // 2, f % 2], own_sem.at[NC + c]
        ).wait()
        for i in range(2 * JC):
            hh, jj = i // JC, i % JC
            lanes = pl.ds(HALF + (c * 2 * JC + i) * HD, HD)
            att[g, :, lanes] = orecv[c, :, hh, pl.ds(jj * GP, GP), :].reshape(ROWS, HD)
        temporal_block(c).start()

    arrive(0)
    attend(0)
    arrive(1)
    for part in range(3):
        wait_bytes(wb.at[part, 0, pl.ds(0, 3)], w2r.at[part])
    post_direct(0, 0)
    post_direct(1, 0)
    post_direct(2, 0)
    post_direct(0, 1)
    post_direct(1, 1)
    post_direct(2, 1)
    attend(1)
    pass_on(0, 0)
    pass_on(1, 0)
    pass_on(2, 0)
    post_direct(0, 2)
    post_direct(1, 2)
    post_direct(2, 2)
    post_direct(0, 3)
    collect(0)
    pass_on(0, 1)
    pass_on(1, 1)
    pass_on(2, 1)
    post_direct(1, 3)
    post_direct(2, 3)
    collect(1)
    hid_in.wait()
    hid_out.wait_recv()
    att_s.wait_recv()
    for c in range(NC):
        temporal_block(c).wait_recv()

    def project(r, carry):
        @pl.when((r == 2) | (r == 3))
        def _():
            for part in (1, 2):
                pass_on(part, r)

        @pl.when(r == 2)
        def _():
            for k in range(2, 4):
                pass_on(0, k)

        for part in (1, 2):
            arrived_far(part, r - 1)

        @pl.when(r == 4)
        def _():
            for k in range(4):
                arrived_far(0, k)

        plane = plane_of(r - 1)
        for s in range(16):
            for part in range(3):
                wch[pl.ds(s * COLS, COLS), pl.ds(part * PART, PART)] = wb[
                    part, plane, s // 4, s % 4
                ]
        near = pl.ds(pl.multiple_of(plane * PLANE, HD), PLANE)
        far = pl.ds(pl.multiple_of(g * HALF + plane * PLANE, HD), PLANE)
        for b in range(2):
            projected = dot(att[b], wch[...], NTDOT)
            mixed = (
                hid[b, :, near].astype(jnp.float32) + gate[pl.ds(b, 1), far] * projected
            ).astype(jnp.bfloat16)
            rows = pl.ds(b * ROWS, ROWS)
            zacc[:, rows] += dot(ft[b, :, near], mixed, NTDOT)
            wide = mixed.astype(jnp.float32)
            square = wide * wide
            sacc[rows, :] += square[:, :128] + square[:, 128:256] + square[:, 256:]
        return carry

    lax.fori_loop(1, 5, project, 0)

    squares = jnp.sum(jnp.transpose(sacc[...]), axis=0, keepdims=True)
    for base in (32, 80):
        block = zacc[pl.ds(base, 8), :]
        pick = lax.broadcasted_iota(jnp.int32, block.shape, 0) == 1
        zacc[pl.ds(base, 8), :] = jnp.where(pick, squares, block)
    zsend = remote(zacc.at[pl.ds(48, 48)], zrecv, part_s.at[4], part_r.at[4], partner)
    zsend.start()
    hid_out.wait_send()
    att_s.wait_send()
    for c in w1 + w2:
        c.wait_send()
    for c in range(NC):
        temporal_block(c).wait_send()
        wait_bytes(recv.at[c, pl.ds(0, FRAMES - 1)], qs_sem.at[c])
        wait_bytes(osend.at[c, pl.ds(0, FRAMES - 1)], os_sem.at[c])

    def drain(r, carry):
        for part in range(3):
            for way in range(2):
                direct(part, r, way).wait_send()
                forward(part, r, way).wait_send()
        return carry

    lax.fori_loop(0, 4, drain, 0)

    zsend.wait_recv()
    velocity = []
    for b in range(2):
        cols = pl.ds(b * ROWS, ROWS)
        total = zacc[pl.ds(0, 40), cols] + zrecv[pl.ds(0, 40), cols]
        mean = total[32:33] * (1.0 / D)
        square = total[33:34] * (1.0 / D)
        velocity.append(
            (total[:32] - mean * consts[b, 0, :, 0:1])
            * lax.rsqrt(square - mean * mean + norm_eps)
            + consts[b, 1, :, 0:1]
        )
    out[...] = velocity[1] + guidance * (velocity[0] - velocity[1])
    zsend.wait_send()


def per_device(
    head_labels,
    queries,
    key_heads,
    value_heads,
    hidden_state,
    gate_scale,
    out_weight,
    final_scale,
    final_shift,
    final_weight,
    latent,
):
    anyspace = pl.BlockSpec(memory_space=pl.ANY)
    vmem = pl.BlockSpec(memory_space=pltpu.VMEM)
    smem = pl.BlockSpec(memory_space=pltpu.SMEM)
    bf16, f32 = jnp.bfloat16, jnp.float32
    dma = pltpu.SemaphoreType.DMA
    guided = pl.pallas_call(
        kernel,
        out_shape=jax.ShapeDtypeStruct((OUT_CH // 2, ROWS), f32),
        in_specs=[smem] + [anyspace] * 5 + [vmem] * 4,
        out_specs=vmem,
        scratch_shapes=[
            pltpu.VMEM((H, ROWS, HD), bf16),
            pltpu.VMEM((H, ROWS, HD), bf16),
            pltpu.VMEM((H, ROWS, HD), bf16),
            pltpu.VMEM((NC, FRAMES // 2, 2, QROWS, HD), bf16),
            pltpu.VMEM((NC, FRAMES, QROWS, HD), bf16),
            pltpu.VMEM((NC, FRAMES, OROWS, HD), bf16),
            pltpu.VMEM((NC, FRAMES // 2, 2, OROWS, HD), bf16),
            pltpu.VMEM((2, ROWS, D), bf16),
            pltpu.VMEM((H, COLS, HD), bf16),
            pltpu.VMEM((3, 4, 4, 4, COLS, PART), bf16),
            pltpu.VMEM((PLANE, D), bf16),
            pltpu.VMEM((2, ROWS, HALF), bf16),
            pltpu.VMEM((3, 4, GP, GP, HD), bf16),
            pltpu.VMEM((4, GP, GP, HD), bf16),
            pltpu.VMEM((2, 96, HALF), bf16),
            pltpu.VMEM((2, 2, 32, HD), f32),
            pltpu.VMEM((96, 2 * ROWS), f32),
            pltpu.VMEM((2 * ROWS, HD), f32),
            pltpu.VMEM((48, 2 * ROWS), f32),
            dma((5,)), dma((2 * NC,)),
            dma((NC,)), dma((NC,)), dma((NC,)), dma((NC,)),
            dma((9,)), dma((3,)), dma((9,)), dma((3,)),
            dma((3, 4, 4)), dma((3, 4, 4)),
            dma((5,)), dma((5,)),
            pltpu.SemaphoreType.REGULAR,
            pltpu.SMEM((H,), jnp.int32),
            pltpu.VMEM((GP * GP, GP * GP), bf16),
        ],
        compiler_params=pltpu.CompilerParams(
            collective_id=0, has_side_effects=True, vmem_limit_bytes=62 * 2**20
        ),
        cost_estimate=pl.CostEstimate(
            flops=16 * 10**9, bytes_accessed=20 * 10**6, transcendentals=4 * 10**6
        ),
        name="guided_layer",
    )(
        head_labels, queries, key_heads, value_heads, hidden_state,
        out_weight.T, final_weight.T, gate_scale, final_scale, final_shift,
    )
    return (latent.T - euler_step * guided).T


def solution(mesh):
    placed = (
        P(),
        P("guide", "frame", None),
        P("guide", "frame", None),
        P("guide", "frame", None),
        P("guide", "frame", None),
        P(),
        P(None, ("guide", "frame")),
        P(),
        P(),
        P(),
        P("frame", "guide"),
    )
    return jax.shard_map(
        per_device, mesh=mesh, in_specs=placed, out_specs=P("frame", "guide"), check_vma=False
    )
```
